256 devices in a mesh: space: 32 (over x, y, core), mem: 8 (over z).
Axes of the slice: x: 4, y: 4, z: 8, core: 2. Of those that a mesh axis runs over, the one named last changes fastest.
Arguments:
- ensemble: bfloat16 [128, 16384, 128], P('mem', 'space'), may hold values from -6 to 6
- obs_count: int32 [1024], P('space'), may hold values from 0 to 256, as said below
- obs_index: int32 [1024, 256], P('space'), may hold values from 0 to 2047
- obs_value: bfloat16 [1024, 256], P('space'), may hold values from -12 to 12
- obs_rinv: bfloat16 [1024, 256], P('space'), may hold values from 0.099609375 to 1
Outputs:
- analysis: bfloat16 [128, 16384, 128], P('mem', 'space')
The draws below stay inside these ranges and needn't reach their ends.
Inputs may be any that keep to these rules, and one draw needn't show every extreme that they name: `obs_count`: in each tile (32 consecutive entries) some blocks have a count of 64 or more and the others 0. The numbers of such blocks in a tile are 32, 8, 6, 5, 4, 4, 3, 2, each number held by 4 tiles, so that the tiles hold 256 such blocks in all. Every tile has a block with a count of exactly 256.
All inputs are finite; a program needn't handle non-finite values.
Results may differ from the reference program's by a relative error of at most 0.011.
Values may be sent and summed in bfloat16 or wider, within the bound.
No kernel may reach another device: no remote copies, remote signals or barrier semaphores. Data moves between devices by JAX's collectives and lax.ppermute only.
A program may use at most 128 MiB of HBM per device.

```python
import math
import jax
import jax.numpy as jnp
from jax import lax

MEMBERS = 128
STATE = 128
OBS = 256
SWEEPS = 8
NB = 32
CB = 16
TILES = 32
BLOCKS = 1024
COLUMNS = 16384


def tile_order(order_key):
    return jax.random.permutation(order_key, NB)


def draw_obs_count(key, part):
    key = jax.random.fold_in(key, 7)
    key_tiles, key_order, key_sizes = jax.random.split(key, 3)
    pattern = jnp.array([32, 8, 6, 5, 4, 4, 3, 2], jnp.int32) * (NB // 32)
    tile_loads = jax.random.permutation(key_tiles, jnp.tile(pattern, TILES // 8))
    order_keys = jax.random.split(key_order, TILES)
    orders = jax.vmap(tile_order)(order_keys).astype(jnp.int32)
    positions = jnp.argsort(orders, axis=1, stable=True).astype(jnp.int32)
    sizes = jax.random.randint(key_sizes, (TILES, NB), OBS // 4, OBS + 1).astype(jnp.int32)
    counts = jnp.where(positions == 0, OBS, sizes)
    counts = jnp.where(positions < tile_loads[:, None], counts, 0)
    return counts.reshape(-1).astype(jnp.int32)


def plant(entries, key, smallest, top_value):
    longest = entries.shape.index(max(entries.shape))
    spots = []
    for shift in (0, 1):
        where = [jax.random.randint(jax.random.fold_in(key, axis), (), 0, length) for axis, length in enumerate(entries.shape)]
        where[longest] = (where[longest] + shift) % entries.shape[longest]
        spots.append(tuple(where))
    return entries.at[spots[0]].set(smallest).at[spots[1]].set(top_value)


def block_levels(stream_key, extent, cuts, low, largest):
    def one(position, shards_of):
        steps = jax.random.uniform(jax.random.fold_in(jax.random.fold_in(stream_key, 6), position), (shards_of,), jnp.float32, low / len(cuts), largest / len(cuts))
        return jnp.repeat(jnp.exp(steps), extent[position] // shards_of).reshape((-1,) + (1,) * (len(extent) - position - 1))

    factor_of = one(*cuts[0])
    for cut in cuts[1:]:
        factor_of = factor_of * one(*cut)
    return factor_of


def normal_values(own_key, extent, scale, bound, shards=(), held_as=jnp.bfloat16):
    gain = block_levels(own_key, extent, shards, -0.22, 0.18) if shards else 1.0
    entries = jax.random.normal(own_key, extent, jnp.float32) * scale * gain
    return jnp.minimum(jnp.maximum(entries, -bound), bound).astype(held_as)


def setup_inputs(seed: int = 0) -> dict:
    streams_of = jax.random.split(jax.random.key(seed), 6)
    return {
        "ensemble": normal_values(streams_of[0], (MEMBERS, COLUMNS, STATE), 1.0, 6.0, ((0, 8), (1, 32))),
        "obs_count": draw_obs_count(jax.random.fold_in(streams_of[5], 71), 0),
        "obs_index": plant(jax.random.randint(streams_of[2], (BLOCKS, OBS), 0, CB * STATE), jax.random.fold_in(streams_of[2], 1), 0, (CB * STATE) - 1).astype(jnp.int32),
        "obs_value": normal_values(streams_of[3], (BLOCKS, OBS), 2.0, 12.0, ((0, 32),)),
        "obs_rinv": jnp.clip(jnp.exp(math.log(1.0) - 2.306499 * jax.random.uniform(streams_of[4], (BLOCKS, OBS), jnp.float32) ** block_levels(streams_of[4], (BLOCKS, OBS), ((0, 32),), -0.2, 0.2)), 0.099609375, 1.0).astype(jnp.bfloat16),
    }


top_precision = lax.Precision.HIGHEST

def transform(obs_full, rinv_part, innov_part):
    member_total = obs_full.shape[0]
    weighted = (obs_full.astype(jnp.float32) * rinv_part.astype(jnp.float32)[None, :, :]).astype(jnp.bfloat16)
    identity = jnp.eye(member_total, dtype=jnp.float32)
    gram_matrix = jnp.einsum('ktp,jtp->tkj', weighted.astype(jnp.float32), obs_full.astype(jnp.float32), precision=top_precision)
    gram_matrix = gram_matrix + (member_total - 1.0) * identity
    drive_vec = jnp.einsum('ktp,tp->tk', weighted.astype(jnp.float32), innov_part.astype(jnp.float32), precision=top_precision)
    trace_scale = lax.optimization_barrier(jnp.sum(gram_matrix * identity, axis=(1, 2)))
    y_iter = gram_matrix / trace_scale[:, None, None]
    z_iter = jnp.broadcast_to(identity, gram_matrix.shape)
    for sweep_index in range(SWEEPS):
        t_step = 1.5 * identity - 0.5 * jnp.einsum('tij,tjk->tik', z_iter, y_iter, precision=top_precision)
        y_iter = jnp.einsum('tij,tjk->tik', y_iter, t_step, precision=top_precision)
        z_iter = jnp.einsum('tij,tjk->tik', t_step, z_iter, precision=top_precision)
    inv_root = z_iter / jnp.sqrt(trace_scale)[:, None, None]
    half_step = jnp.einsum('tij,tj->ti', inv_root, drive_vec, precision=top_precision)
    mean_shift = jnp.einsum('tij,tj->ti', inv_root, half_step, precision=top_precision)
    return (math.sqrt(member_total - 1.0) * inv_root + mean_shift[:, :, None]).astype(jnp.bfloat16)

def analyse(block_ens, spot_vals, rinv_part, obs_part):
    member_total = block_ens.shape[0]
    col_mean = lax.optimization_barrier(jnp.sum(block_ens.astype(jnp.float32), axis=0)) / member_total
    col_pert = (block_ens.astype(jnp.float32) - col_mean).astype(jnp.bfloat16)
    spot_mean = lax.optimization_barrier(jnp.sum(spot_vals.astype(jnp.float32), axis=0)) / member_total
    obs_pert = (spot_vals.astype(jnp.float32) - spot_mean).astype(jnp.bfloat16)
    innov = (obs_part.astype(jnp.float32) - spot_mean).astype(jnp.bfloat16)
    weights = transform(obs_pert, rinv_part, innov)
    increment = jnp.einsum('ktcs,tki->itcs', col_pert.astype(jnp.float32), weights.astype(jnp.float32), precision=top_precision)
    return (col_mean + increment).astype(jnp.bfloat16)

def tile_step(tile_items):
    return analyse(tile_items[0], tile_items[1], tile_items[2], tile_items[3])

def reference(ensemble, obs_count, obs_index, obs_value, obs_rinv):
    flat_ens = ensemble.reshape(MEMBERS, BLOCKS, CB * STATE)
    spot_index = jnp.broadcast_to(obs_index[None, :, :], (MEMBERS, BLOCKS, OBS))
    spot_vals = jnp.take_along_axis(flat_ens, spot_index, axis=2)
    slot_iota = jnp.arange(OBS, dtype=jnp.int32)
    rinv_used = jnp.where(slot_iota[None, :] < obs_count[:, None], obs_rinv, jnp.zeros_like(obs_rinv))
    tile_ens = ensemble.reshape(MEMBERS, TILES, NB, CB, STATE).transpose(1, 0, 2, 3, 4)
    tile_spots = spot_vals.reshape(MEMBERS, TILES, NB, OBS).transpose(1, 0, 2, 3)
    tile_rinv = rinv_used.reshape(TILES, NB, OBS)
    tile_obs = obs_value.reshape(TILES, NB, OBS)
    analysed = lax.map(tile_step, (tile_ens, tile_spots, tile_rinv, tile_obs))
    result = analysed.transpose(1, 0, 2, 3, 4).reshape(MEMBERS, COLUMNS, STATE)
    live_cols = jnp.repeat(obs_count > 0, CB)
    return jnp.where(live_cols[None, :, None], result, ensemble)
```

```python
import functools
import math

import jax
import jax.numpy as jnp
from jax import lax
from jax.experimental import pallas as pl
from jax.experimental.pallas import tpu as pltpu
from jax.sharding import PartitionSpec as P

SWEEPS = 8
F32 = jnp.float32
BF16 = jnp.bfloat16


def split(x):
    high = x.astype(BF16)
    low = (x - high.astype(F32)).astype(BF16)
    return high, low


def as_left(parts):
    pieces = [split(p) for p in parts]
    return jnp.concatenate([jnp.concatenate([h, l], axis=1) for h, l in pieces], axis=0)


def as_right(x):
    high, low = split(x)
    row = jnp.concatenate([high, low], axis=1)
    return jnp.concatenate([row, row], axis=0)


def product(left, right):
    full = jnp.dot(left, right, preferred_element_type=F32)
    half = full.shape[1] // 2
    return full[:, :half] + full[:, half:]


def analyse_kernel(nb, cols, idx_ref, val_ref, rinv_ref, *refs):
    peers = 8
    chunks, outs, scratch = refs[:peers], refs[peers : 2 * peers], refs[2 * peers :]
    full, raw, pert = scratch
    share = chunks[0].shape[0]
    members = share * peers
    state = chunks[0].shape[2]
    slots = idx_ref.shape[1]
    cells = cols * state
    row_iota = lax.broadcasted_iota(jnp.int32, (members, members), 0)
    col_iota = lax.broadcasted_iota(jnp.int32, (members, members), 1)
    identity = (row_iota == col_iota).astype(F32)
    means, starts, scales, ws, zs, us = [], [], [], [], [], []
    for q in range(nb):
        total = jnp.zeros((cols, state), F32)
        for d in range(peers):
            x = chunks[d][:, q * cols : (q + 1) * cols, :].astype(F32)
            full[q, d * share : (d + 1) * share] = x
            total = total + jnp.sum(x, axis=0)
        means.append(total / members)
    for q in range(nb):
        for c in range(cols):
            x = full[q, :, c, :]
            raw[q, :, c * state : (c + 1) * state] = x.astype(BF16)
            pert[q, :, c * state : (c + 1) * state] = (x - means[q][c : c + 1, :]).astype(BF16)
    for q in range(nb):
        idx = idx_ref[q : q + 1, :]
        spot_col = idx // state
        spot_state = idx - spot_col * state
        state_hit = (
            lax.broadcasted_iota(jnp.int32, (state, slots), 0) == spot_state
        ).astype(F32).astype(BF16)
        table = jnp.concatenate(
            [state_hit * (spot_col == c).astype(F32).astype(BF16) for c in range(cols)], axis=0
        )
        spots = jnp.dot(raw[q], table, preferred_element_type=F32)
        spot_mean = jnp.sum(spots, axis=0, keepdims=True) / members
        obs_pert = (spots - spot_mean).astype(BF16)
        innov = (val_ref[q : q + 1, :] - spot_mean).astype(BF16)
        weighted = (obs_pert.astype(F32) * rinv_ref[q : q + 1, :]).astype(BF16)
        left = jnp.concatenate([obs_pert, jnp.broadcast_to(innov, (16, slots))], axis=0)
        both = lax.dot_general(
            left, weighted, (((1,), (1,)), ((), ())), preferred_element_type=F32
        )
        gram = both[:members] + (members - 1.0) * identity
        scale = jnp.sum(jnp.sum(gram * identity, axis=1, keepdims=True), axis=0, keepdims=True)
        scales.append(scale)
        ws.append(gram / scale)
        us.append(both[members:])
    for q in range(nb):
        w, u = ws[q], us[q]
        right = as_right(w)
        first = product(as_left([w, u]), right)
        second = product(as_left([first[:members], first[members:]]), right)
        zs.append(1.5 * identity - 0.5 * w)
        ws[q] = 2.25 * w - 1.5 * first[:members] + 0.25 * second[:members]
        us[q] = 2.25 * u - 1.5 * first[members:] + 0.25 * second[members:]
    for sweep in range(1, SWEEPS - 1):
        for q in range(nb):
            w, z, u = ws[q], zs[q], us[q]
            right = as_right(w)
            first = product(as_left([w, u, z]), right)
            ww, uw, zw = first[:members], first[members : members + 16], first[members + 16 :]
            second = product(as_left([ww, uw]), right)
            zs[q] = 1.5 * z - 0.5 * zw
            ws[q] = 2.25 * w - 1.5 * ww + 0.25 * second[:members]
            us[q] = 2.25 * u - 1.5 * uw + 0.25 * second[members:]
    for q in range(nb):
        w, z, u = ws[q], zs[q], us[q]
        right = as_right(w)
        first = product(as_left([z, u]), right)
        uw = first[members:]
        second = product(as_left([uw]), right)
        z = 1.5 * z - 0.5 * first[:members]
        u = 2.25 * u - 1.5 * uw + 0.25 * second
        scale = scales[q]
        weights = (math.sqrt(members - 1.0) / jnp.sqrt(scale)) * z + u[:1] / scale
        increment = jnp.dot(weights.astype(BF16), pert[q], preferred_element_type=F32)
        for c in range(cols):
            full[q, :, c, :] = (
                increment[:, c * state : (c + 1) * state] + means[q][c : c + 1, :]
            )
    for q in range(nb):
        for d in range(peers):
            outs[d][:, q * cols : (q + 1) * cols, :] = full[
                q, d * share : (d + 1) * share
            ].astype(BF16)


def analyse(nb, cols, idx, val, rinv, chunks):
    share, _, state = chunks[0].shape
    members = share * len(chunks)
    return pl.pallas_call(
        functools.partial(analyse_kernel, nb, cols),
        out_shape=[jax.ShapeDtypeStruct(c.shape, c.dtype) for c in chunks],
        in_specs=[pl.BlockSpec(memory_space=pltpu.VMEM)] * (3 + len(chunks)),
        out_specs=[pl.BlockSpec(memory_space=pltpu.VMEM)] * len(chunks),
        scratch_shapes=[
            pltpu.VMEM((nb, members, cols, state), F32),
            pltpu.VMEM((nb, members, cols * state), BF16),
            pltpu.VMEM((nb, members, cols * state), BF16),
        ],
        compiler_params=pltpu.CompilerParams(vmem_limit_bytes=48 * 1024 * 1024),
        cost_estimate=pl.CostEstimate(
            flops=nb * 500_000_000, bytes_accessed=nb * 1_048_576, transcendentals=0
        ),
    )(idx, val, rinv, *chunks)


def rows_for(obs_count, obs_index, obs_value, obs_rinv, start, nb):
    slots = obs_index.shape[1]
    cut = lambda a: lax.dynamic_slice_in_dim(a, start, nb, 0)
    used = lax.broadcasted_iota(jnp.int32, (nb, slots), 1) < cut(obs_count)[:, None]
    rinv = jnp.where(used, cut(obs_rinv).astype(F32), 0.0)
    return cut(obs_index), cut(obs_value).astype(F32), rinv


def all_kernel(info, *refs):
    peers = 8
    chunks, out, sems = refs[:peers], refs[peers], refs[peers + 1]
    width = chunks[0].shape[1]
    copies = []
    for d in range(peers):
        at = pl.multiple_of(lax.rem(info[0] + d, peers) * width, width)
        copies.append(
            pltpu.make_async_copy(chunks[d], out.at[:, pl.ds(at, width), :], sems.at[d])
        )
    for copy in copies:
        copy.start()
    for copy in copies:
        copy.wait()


def some_kernel(info, ens, *refs):
    peers = 8
    chunks, out, sems = refs[:peers], refs[peers], refs[peers + 1]
    cols = chunks[0].shape[1]
    blocks = out.shape[1] // cols
    copies = []
    for b in range(blocks):
        at = b * cols
        copies.append((
            info[2 + peers + b] <= 0,
            pltpu.make_async_copy(
                ens.at[:, pl.ds(at, cols), :], out.at[:, pl.ds(at, cols), :], sems.at[b]
            ),
        ))
    for d in range(peers):
        turn = lax.rem(info[0] + d, peers)
        at = pl.multiple_of(info[2 + turn] * cols, cols)
        copies.append((
            turn < info[1],
            pltpu.make_async_copy(
                chunks[d], out.at[:, pl.ds(at, cols), :], sems.at[blocks + d]
            ),
        ))
    for wanted, copy in copies:
        pl.when(wanted)(copy.start)
    for wanted, copy in copies:
        pl.when(wanted)(copy.wait)


def assemble(kernel, info, arrays, shape, sems):
    return pl.pallas_call(
        kernel,
        out_shape=jax.ShapeDtypeStruct(shape, BF16),
        in_specs=[pl.BlockSpec(memory_space=pltpu.SMEM)]
        + [pl.BlockSpec(memory_space=pl.ANY)] * len(arrays),
        out_specs=pl.BlockSpec(memory_space=pl.ANY),
        scratch_shapes=[pltpu.SemaphoreType.DMA((sems,))],
    )(info, *arrays)


def shards(ensemble, obs_count, obs_index, obs_value, obs_rinv):
    share, columns, state = ensemble.shape
    blocks = obs_count.shape[0]
    cols = columns // blocks
    peers = lax.axis_size("mem")
    me = lax.axis_index("mem")
    live = obs_count > 0
    live_int = live.astype(jnp.int32)
    load = jnp.sum(live_int)

    def shifted(x, d):
        if d == 0:
            return x
        return lax.ppermute(x, "mem", [(i, (i + d) % peers) for i in range(peers)])

    def whole():
        nb = blocks // peers
        width = nb * cols
        info = me[None].astype(jnp.int32)
        sent = [
            lax.dynamic_slice_in_dim(ensemble, lax.rem(me + d, peers) * width, width, 1)
            for d in range(peers)
        ]
        got = [shifted(sent[d], d) for d in range(peers)]
        rows = rows_for(obs_count, obs_index, obs_value, obs_rinv, me * nb, nb)
        done = analyse(nb, cols, *rows, got)
        back = [shifted(done[d], peers - d if d else 0) for d in range(peers)]
        return assemble(all_kernel, info, back, ensemble.shape, peers)

    def part():
        rank = jnp.cumsum(live_int) - 1
        turns = jnp.arange(peers, dtype=jnp.int32)
        hits = (rank[None, :] == turns[:, None]) & live[None, :]
        listing = jnp.sum(
            jnp.where(hits, jnp.arange(blocks, dtype=jnp.int32)[None, :], 0), axis=1
        )
        info = jnp.concatenate([me[None].astype(jnp.int32), load[None], listing, obs_count])
        sent = [
            lax.dynamic_slice_in_dim(
                ensemble, listing[lax.rem(me + d, peers)] * cols, cols, 1
            )
            for d in range(peers)
        ]
        got = [shifted(sent[d], d) for d in range(peers)]
        rows = rows_for(obs_count, obs_index, obs_value, obs_rinv, listing[me], 1)
        done = analyse(1, cols, *rows, got)
        back = [shifted(done[d], peers - d if d else 0) for d in range(peers)]
        return assemble(some_kernel, info, [ensemble] + back, ensemble.shape, blocks + peers)

    return lax.cond(load > peers, whole, part)


def solution(mesh):
    return jax.shard_map(
        shards,
        mesh=mesh,
        in_specs=(
            P("mem", "space", None),
            P("space"),
            P("space", None),
            P("space", None),
            P("space", None),
        ),
        out_specs=P("mem", "space", None),
        check_vma=False,
    )
```

```python
import functools
import math

import jax
import jax.numpy as jnp
from jax import lax
from jax.experimental import pallas as pl
from jax.experimental.pallas import tpu as pltpu
from jax.sharding import PartitionSpec as P

SWEEPS = 8
F32 = jnp.float32
BF16 = jnp.bfloat16


def split(x):
    high = x.astype(BF16)
    low = (x - high.astype(F32)).astype(BF16)
    return high, low


def as_left(parts):
    pieces = [split(p) for p in parts]
    return jnp.concatenate([jnp.concatenate([h, l], axis=1) for h, l in pieces], axis=0)


def as_right(x):
    high, low = split(x)
    row = jnp.concatenate([high, low], axis=1)
    return jnp.concatenate([row, row], axis=0)


def product(left, right):
    full = jnp.dot(left, right, preferred_element_type=F32)
    half = full.shape[1] // 2
    return full[:, :half] + full[:, half:]


def analyse_kernel(nb, cols, idx_ref, val_ref, rinv_ref, *refs):
    chunks, outs, both_ref = refs[:PEERS], refs[PEERS : 2 * PEERS], refs[2 * PEERS]
    share = chunks[0].shape[0]
    members = share * PEERS
    state = chunks[0].shape[2]
    slots = idx_ref.shape[1]
    tall = share * cols
    row_iota = lax.broadcasted_iota(jnp.int32, (members, members), 0)
    col_iota = lax.broadcasted_iota(jnp.int32, (members, members), 1)
    identity = (row_iota == col_iota).astype(F32)
    tall_row = lax.broadcasted_iota(jnp.int32, (tall, tall), 0)
    tall_col = lax.broadcasted_iota(jnp.int32, (tall, tall), 1)
    swap = (tall_col == (tall_row % share) * cols + tall_row // share).astype(F32).astype(BF16)
    ones = jnp.ones((16, members), BF16)
    scales, ws, zs, us = [], [], [], []
    for q in range(nb):
        for d in range(0, PEERS, 2):
            pair = jnp.concatenate(
                [
                    chunks[e][:, q * cols : (q + 1) * cols, :].reshape(tall, state)
                    for e in (d, d + 1)
                ],
                axis=1,
            )
            turned = jnp.dot(swap, pair, preferred_element_type=F32).astype(BF16)
            for e in (0, 1):
                for c in range(cols):
                    both_ref[
                        q, (d + e) * share : (d + e + 1) * share, c * state : (c + 1) * state
                    ] = turned[c * share : (c + 1) * share, e * state : (e + 1) * state]
    for q in range(nb):
        raw = both_ref[q, :members]
        mean = jnp.dot(ones, raw, preferred_element_type=F32) / members
        high, low = split(mean)
        rest = (mean - high.astype(F32) - low.astype(F32)).astype(BF16)
        turn = lax.broadcasted_iota(jnp.int32, mean.shape, 0) % 3
        pick = lambda p: p.astype(F32)
        both_ref[q, members:] = jnp.where(
            turn == 0, pick(high), jnp.where(turn == 1, pick(low), pick(rest))
        ).astype(BF16)
    for q in range(nb):
        idx = idx_ref[q : q + 1, :]
        spot_col = idx // state
        spot_state = idx - spot_col * state
        state_hit = (
            lax.broadcasted_iota(jnp.int32, (state, slots), 0) == spot_state
        ).astype(F32).astype(BF16)
        table = jnp.concatenate(
            [state_hit * (spot_col == c).astype(F32).astype(BF16) for c in range(cols)], axis=0
        )
        spots = jnp.dot(both_ref[q, :members], table, preferred_element_type=F32)
        spot_mean = jnp.sum(spots, axis=0, keepdims=True) / members
        obs_pert = (spots - spot_mean).astype(BF16)
        innov = (val_ref[q : q + 1, :] - spot_mean).astype(BF16)
        weighted = (obs_pert.astype(F32) * rinv_ref[q : q + 1, :]).astype(BF16)
        left = jnp.concatenate([obs_pert, jnp.broadcast_to(innov, (16, slots))], axis=0)
        both = lax.dot_general(
            left, weighted, (((1,), (1,)), ((), ())), preferred_element_type=F32
        )
        gram = both[:members] + (members - 1.0) * identity
        scale = jnp.sum(jnp.sum(gram * identity, axis=1, keepdims=True), axis=0, keepdims=True)
        scales.append(scale)
        ws.append(gram / scale)
        us.append(both[members:])
    for q in range(nb):
        w, u = ws[q], us[q]
        right = as_right(w)
        first = product(as_left([w, u]), right)
        second = product(as_left([first[:members], first[members:]]), right)
        zs.append(1.5 * identity - 0.5 * w)
        ws[q] = 2.25 * w - 1.5 * first[:members] + 0.25 * second[:members]
        us[q] = 2.25 * u - 1.5 * first[members:] + 0.25 * second[members:]
    for sweep in range(1, SWEEPS - 1):
        for q in range(nb):
            w, z, u = ws[q], zs[q], us[q]
            right = as_right(w)
            first = product(as_left([w, u, z]), right)
            ww, uw, zw = first[:members], first[members : members + 16], first[members + 16 :]
            second = product(as_left([ww, uw]), right)
            zs[q] = 1.5 * z - 0.5 * zw
            ws[q] = 2.25 * w - 1.5 * ww + 0.25 * second[:members]
            us[q] = 2.25 * u - 1.5 * uw + 0.25 * second[members:]
    for q in range(nb):
        w, z, u = ws[q], zs[q], us[q]
        right = as_right(w)
        first = product(as_left([z, u]), right)
        uw = first[members:]
        second = product(as_left([uw]), right)
        z = 1.5 * z - 0.5 * first[:members]
        u = 2.25 * u - 1.5 * uw + 0.25 * second
        scale = scales[q]
        weights = ((math.sqrt(members - 1.0) / jnp.sqrt(scale)) * z + u[:1] / scale).astype(BF16)
        spare = 1.0 - jnp.sum(weights.astype(F32), axis=1, keepdims=True)
        high, low = split(spare)
        lane = lax.broadcasted_iota(jnp.int32, (members, 16), 1)
        tail = jnp.where(
            lane < 3, high.astype(F32), jnp.where(lane < 6, low.astype(F32), 0.0)
        ).astype(BF16)
        left = jnp.concatenate([weights, tail], axis=1)
        result = jnp.dot(left, both_ref[q], preferred_element_type=F32).astype(BF16)
        for d in range(0, PEERS, 2):
            pair = jnp.concatenate(
                [
                    jnp.concatenate(
                        [
                            result[e * share : (e + 1) * share, c * state : (c + 1) * state]
                            for c in range(cols)
                        ],
                        axis=0,
                    )
                    for e in (d, d + 1)
                ],
                axis=1,
            )
            turned = jnp.dot(swap, pair, preferred_element_type=F32).astype(BF16)
            for e in (0, 1):
                outs[d + e][:, q * cols : (q + 1) * cols, :] = turned[
                    :, e * state : (e + 1) * state
                ].reshape(share, cols, state)


def analyse(nb, cols, idx, val, rinv, chunks):
    share, _, state = chunks[0].shape
    members = share * len(chunks)
    return pl.pallas_call(
        functools.partial(analyse_kernel, nb, cols),
        out_shape=[jax.ShapeDtypeStruct(c.shape, c.dtype) for c in chunks],
        in_specs=[pl.BlockSpec(memory_space=pltpu.VMEM)] * (3 + len(chunks)),
        out_specs=[pl.BlockSpec(memory_space=pltpu.VMEM)] * len(chunks),
        scratch_shapes=[pltpu.VMEM((nb, members + 16, cols * state), BF16)],
        compiler_params=pltpu.CompilerParams(vmem_limit_bytes=24 * 1024 * 1024),
        cost_estimate=pl.CostEstimate(
            flops=nb * 2_000_000_000, bytes_accessed=nb * 1_048_576, transcendentals=0
        ),
    )(idx, val, rinv, *chunks)


PEERS = 8
PARTS = 2


def plan_kernel(blocks, me, count, info, load):
    turn = jnp.int32(0)
    for r in range(PEERS):
        info[2 + r] = 0
    for b in range(blocks):
        seen = count[b]
        info[2 + PEERS + b] = seen

        @pl.when((seen > 0) & (turn < PEERS))
        def _():
            info[2 + turn] = b

        turn = turn + (seen > 0).astype(jnp.int32)
    info[0] = me[0]
    info[1] = turn
    load[0] = turn


def make_plan(me, obs_count):
    blocks = obs_count.shape[0]
    smem = pl.BlockSpec(memory_space=pltpu.SMEM)
    return pl.pallas_call(
        functools.partial(plan_kernel, blocks),
        out_shape=[
            jax.ShapeDtypeStruct((2 + PEERS + blocks,), jnp.int32),
            jax.ShapeDtypeStruct((1,), jnp.int32),
        ],
        in_specs=[smem] * 2,
        out_specs=[smem] * 2,
    )(me, obs_count)


def pack_kernel(nb, base, cols, listed, info, ens, idx, val, rinv, *refs):
    outs = refs[:PEERS]
    idx_out, val_out, rinv_out, val_all, rinv_all, sems = refs[PEERS:]
    slots = idx.shape[1]
    width = nb * cols
    copies = []
    for d in range(PEERS):
        turn = lax.rem(info[0] + d, PEERS)
        first = info[2 + turn] if listed else base + turn * nb
        at = pl.multiple_of(first * cols, cols)
        copies.append(
            pltpu.make_async_copy(ens.at[:, pl.ds(at, width), :], outs[d], sems.at[d])
        )
    for copy in copies:
        copy.start()
    mine = info[2 + info[0]] if listed else base + info[0] * nb
    slot = lax.broadcasted_iota(jnp.int32, (1, slots), 1)
    val_all[...] = val[...].astype(F32)
    rinv_all[...] = rinv[...].astype(F32)
    for q in range(nb):
        row = pl.ds(mine + q, 1)
        idx_out[q : q + 1, :] = idx[row, :]
        val_out[q : q + 1, :] = val_all[row, :]
        used = slot < info[2 + PEERS + mine + q]
        rinv_out[q : q + 1, :] = jnp.where(used, rinv_all[row, :], 0.0)
    for copy in copies:
        copy.wait()


def pack(nb, base, cols, listed, info, ensemble, idx, val, rinv):
    share, _, state = ensemble.shape
    slots = idx.shape[1]
    smem = pl.BlockSpec(memory_space=pltpu.SMEM)
    vmem = pl.BlockSpec(memory_space=pltpu.VMEM)
    hbm = pl.BlockSpec(memory_space=pl.ANY)
    got = pl.pallas_call(
        functools.partial(pack_kernel, nb, base, cols, listed),
        out_shape=[jax.ShapeDtypeStruct((share, nb * cols, state), BF16)] * PEERS
        + [
            jax.ShapeDtypeStruct((nb, slots), jnp.int32),
            jax.ShapeDtypeStruct((nb, slots), F32),
            jax.ShapeDtypeStruct((nb, slots), F32),
        ],
        in_specs=[smem, hbm, vmem, vmem, vmem],
        out_specs=[vmem] * (PEERS + 3),
        scratch_shapes=[
            pltpu.VMEM(val.shape, F32),
            pltpu.VMEM(rinv.shape, F32),
            pltpu.SemaphoreType.DMA((PEERS,)),
        ],
        compiler_params=pltpu.CompilerParams(vmem_limit_bytes=16 * 1024 * 1024),
    )(info, ensemble, idx, val, rinv)
    return got[:PEERS], got[PEERS:]


def all_kernel(info, *refs):
    chunks, out, sems = refs[:-2], refs[-2], refs[-1]
    width = chunks[0].shape[1]
    copies = []
    for i, chunk in enumerate(chunks):
        turn = lax.rem(info[0] + i % PEERS, PEERS)
        at = pl.multiple_of((i // PEERS * PEERS + turn) * width, width)
        copies.append(
            pltpu.make_async_copy(chunk, out.at[:, pl.ds(at, width), :], sems.at[i])
        )
    for copy in copies:
        copy.start()
    for copy in copies:
        copy.wait()


def some_kernel(info, ens, *refs):
    chunks, out, sems = refs[:PEERS], refs[PEERS], refs[PEERS + 1]
    cols = chunks[0].shape[1]
    blocks = out.shape[1] // cols
    copies = []
    for b in range(blocks):
        at = b * cols
        copies.append((
            info[2 + PEERS + b] <= 0,
            pltpu.make_async_copy(
                ens.at[:, pl.ds(at, cols), :], out.at[:, pl.ds(at, cols), :], sems.at[b]
            ),
        ))
    for d in range(PEERS):
        turn = lax.rem(info[0] + d, PEERS)
        at = pl.multiple_of(info[2 + turn] * cols, cols)
        copies.append((
            turn < info[1],
            pltpu.make_async_copy(
                chunks[d], out.at[:, pl.ds(at, cols), :], sems.at[blocks + d]
            ),
        ))
    for wanted, copy in copies:
        pl.when(wanted)(copy.start)
    for wanted, copy in copies:
        pl.when(wanted)(copy.wait)


def assemble(kernel, info, arrays, chunks, shape, sems):
    hbm = pl.BlockSpec(memory_space=pl.ANY)
    vmem = pl.BlockSpec(memory_space=pltpu.VMEM)
    return pl.pallas_call(
        kernel,
        out_shape=jax.ShapeDtypeStruct(shape, BF16),
        in_specs=[pl.BlockSpec(memory_space=pltpu.SMEM)]
        + [hbm] * len(arrays)
        + [vmem] * len(chunks),
        out_specs=hbm,
        scratch_shapes=[pltpu.SemaphoreType.DMA((sems,))],
    )(info, *arrays, *chunks)


def shards(ensemble, obs_count, obs_index, obs_value, obs_rinv):
    share, columns, state = ensemble.shape
    blocks = obs_count.shape[0]
    cols = columns // blocks
    me = lax.axis_index("mem").astype(jnp.int32)
    info, load = make_plan(me[None], obs_count)

    def shifted(x, d):
        if d == 0:
            return x
        return lax.ppermute(x, "mem", [(i, (i + d) % PEERS) for i in range(PEERS)])

    def run(nb, base, listed):
        sent, rows = pack(
            nb, base, cols, listed, info, ensemble, obs_index, obs_value, obs_rinv
        )
        got = [shifted(sent[d], d) for d in range(PEERS)]
        done = analyse(nb, cols, *rows, got)
        return [shifted(done[d], PEERS - d if d else 0) for d in range(PEERS)]

    def whole():
        back = []
        for part_index in range(PARTS):
            back += run(
                blocks // PEERS // PARTS, part_index * (blocks // PARTS), False
            )
        return assemble(all_kernel, info, [], back, ensemble.shape, PEERS * PARTS)

    def part():
        back = run(1, 0, True)
        return assemble(some_kernel, info, [ensemble], back, ensemble.shape, blocks + PEERS)

    return lax.cond(load[0] > PEERS, whole, part)


def solution(mesh):
    return jax.shard_map(
        shards,
        mesh=mesh,
        in_specs=(
            P("mem", "space", None),
            P("space"),
            P("space", None),
            P("space", None),
            P("space", None),
        ),
        out_specs=P("mem", "space", None),
        check_vma=False,
    )
```

```python
import functools
import math

import jax
import jax.numpy as jnp
from jax import lax
from jax.experimental import pallas as pl
from jax.experimental.pallas import tpu as pltpu
from jax.sharding import PartitionSpec as P

SWEEPS = 8
F32 = jnp.float32
BF16 = jnp.bfloat16


def split(x):
    high = x.astype(BF16)
    low = (x - high.astype(F32)).astype(BF16)
    return high, low


def as_left(parts):
    pieces = [split(p) for p in parts]
    return jnp.concatenate([jnp.concatenate([h, l], axis=1) for h, l in pieces], axis=0)


def as_right(x):
    high, low = split(x)
    row = jnp.concatenate([high, low], axis=1)
    return jnp.concatenate([row, row], axis=0)


def product(left, right):
    full = jnp.dot(left, right, preferred_element_type=F32)
    half = full.shape[1] // 2
    return full[:, :half] + full[:, half:]


def analyse_kernel(nb, cols, idx_ref, val_ref, rinv_ref, chunks, outs, both_ref):
    share = chunks.shape[1]
    members = share * PEERS
    state = chunks.shape[3]
    slots = idx_ref.shape[1]
    tall = share * cols
    row_iota = lax.broadcasted_iota(jnp.int32, (members, members), 0)
    col_iota = lax.broadcasted_iota(jnp.int32, (members, members), 1)
    identity = (row_iota == col_iota).astype(F32)
    tall_row = lax.broadcasted_iota(jnp.int32, (tall, tall), 0)
    tall_col = lax.broadcasted_iota(jnp.int32, (tall, tall), 1)
    swap = (tall_col == (tall_row % share) * cols + tall_row // share).astype(F32).astype(BF16)
    ones = jnp.ones((16, members), BF16)
    scales, ws, zs, us = [], [], [], []
    for q in range(nb):
        for d in range(0, PEERS, 2):
            pair = jnp.concatenate(
                [
                    chunks[e, :, q * cols : (q + 1) * cols, :].reshape(tall, state)
                    for e in (d, d + 1)
                ],
                axis=1,
            )
            turned = jnp.dot(swap, pair, preferred_element_type=F32).astype(BF16)
            for e in (0, 1):
                for c in range(cols):
                    both_ref[
                        q, (d + e) * share : (d + e + 1) * share, c * state : (c + 1) * state
                    ] = turned[c * share : (c + 1) * share, e * state : (e + 1) * state]
    for q in range(nb):
        raw = both_ref[q, :members]
        mean = jnp.dot(ones, raw, preferred_element_type=F32) / members
        high, low = split(mean)
        rest = (mean - high.astype(F32) - low.astype(F32)).astype(BF16)
        turn = lax.broadcasted_iota(jnp.int32, mean.shape, 0) % 3
        pick = lambda p: p.astype(F32)
        both_ref[q, members:] = jnp.where(
            turn == 0, pick(high), jnp.where(turn == 1, pick(low), pick(rest))
        ).astype(BF16)
    for q in range(nb):
        idx = idx_ref[q : q + 1, :]
        spot_col = idx // state
        spot_state = idx - spot_col * state
        state_hit = (
            lax.broadcasted_iota(jnp.int32, (state, slots), 0) == spot_state
        ).astype(F32).astype(BF16)
        table = jnp.concatenate(
            [state_hit * (spot_col == c).astype(F32).astype(BF16) for c in range(cols)], axis=0
        )
        spots = jnp.dot(both_ref[q, :members], table, preferred_element_type=F32)
        spot_mean = jnp.sum(spots, axis=0, keepdims=True) / members
        obs_pert = (spots - spot_mean).astype(BF16)
        innov = (val_ref[q : q + 1, :] - spot_mean).astype(BF16)
        weighted = (obs_pert.astype(F32) * rinv_ref[q : q + 1, :]).astype(BF16)
        left = jnp.concatenate([obs_pert, jnp.broadcast_to(innov, (16, slots))], axis=0)
        both = lax.dot_general(
            left, weighted, (((1,), (1,)), ((), ())), preferred_element_type=F32
        )
        gram = both[:members] + (members - 1.0) * identity
        scale = jnp.sum(jnp.sum(gram * identity, axis=1, keepdims=True), axis=0, keepdims=True)
        scales.append(scale)
        ws.append(gram / scale)
        us.append(both[members:])
    for q in range(nb):
        w, u = ws[q], us[q]
        right = as_right(w)
        first = product(as_left([w, u]), right)
        second = product(as_left([first[:members], first[members:]]), right)
        zs.append(1.5 * identity - 0.5 * w)
        ws[q] = 2.25 * w - 1.5 * first[:members] + 0.25 * second[:members]
        us[q] = 2.25 * u - 1.5 * first[members:] + 0.25 * second[members:]
    for sweep in range(1, SWEEPS - 1):
        for q in range(nb):
            w, z, u = ws[q], zs[q], us[q]
            right = as_right(w)
            first = product(as_left([w, u, z]), right)
            ww, uw, zw = first[:members], first[members : members + 16], first[members + 16 :]
            second = product(as_left([ww, uw]), right)
            zs[q] = 1.5 * z - 0.5 * zw
            ws[q] = 2.25 * w - 1.5 * ww + 0.25 * second[:members]
            us[q] = 2.25 * u - 1.5 * uw + 0.25 * second[members:]
    for q in range(nb):
        w, z, u = ws[q], zs[q], us[q]
        right = as_right(w)
        first = product(as_left([z, u]), right)
        uw = first[members:]
        second = product(as_left([uw]), right)
        z = 1.5 * z - 0.5 * first[:members]
        u = 2.25 * u - 1.5 * uw + 0.25 * second
        scale = scales[q]
        weights = ((math.sqrt(members - 1.0) / jnp.sqrt(scale)) * z + u[:1] / scale).astype(BF16)
        spare = 1.0 - jnp.sum(weights.astype(F32), axis=1, keepdims=True)
        high, low = split(spare)
        lane = lax.broadcasted_iota(jnp.int32, (members, 16), 1)
        tail = jnp.where(
            lane < 3, high.astype(F32), jnp.where(lane < 6, low.astype(F32), 0.0)
        ).astype(BF16)
        left = jnp.concatenate([weights, tail], axis=1)
        result = jnp.dot(left, both_ref[q], preferred_element_type=F32).astype(BF16)
        for d in range(0, PEERS, 2):
            pair = jnp.concatenate(
                [
                    jnp.concatenate(
                        [
                            result[e * share : (e + 1) * share, c * state : (c + 1) * state]
                            for c in range(cols)
                        ],
                        axis=0,
                    )
                    for e in (d, d + 1)
                ],
                axis=1,
            )
            turned = jnp.dot(swap, pair, preferred_element_type=F32).astype(BF16)
            for e in (0, 1):
                outs[d + e, :, q * cols : (q + 1) * cols, :] = turned[
                    :, e * state : (e + 1) * state
                ].reshape(share, cols, state)


def analyse(nb, cols, idx, val, rinv, chunks):
    peers, share, _, state = chunks.shape
    members = share * peers
    vmem = pl.BlockSpec(memory_space=pltpu.VMEM)
    return pl.pallas_call(
        functools.partial(analyse_kernel, nb, cols),
        out_shape=jax.ShapeDtypeStruct(chunks.shape, chunks.dtype),
        in_specs=[vmem] * 4,
        out_specs=vmem,
        scratch_shapes=[pltpu.VMEM((nb, members + 16, cols * state), BF16)],
        compiler_params=pltpu.CompilerParams(vmem_limit_bytes=24 * 1024 * 1024),
        cost_estimate=pl.CostEstimate(
            flops=nb * 2_000_000_000, bytes_accessed=nb * 1_048_576, transcendentals=0
        ),
    )(idx, val, rinv, chunks)


PEERS = 8
PARTS = 1


def plan_kernel(blocks, me, count, info, load):
    turn = jnp.int32(0)
    for r in range(PEERS):
        info[2 + r] = 0
    for b in range(blocks):
        seen = count[b]
        info[2 + PEERS + b] = seen

        @pl.when((seen > 0) & (turn < PEERS))
        def _():
            info[2 + turn] = b

        turn = turn + (seen > 0).astype(jnp.int32)
    info[0] = me[0]
    info[1] = turn
    load[0] = turn


def make_plan(me, obs_count):
    blocks = obs_count.shape[0]
    smem = pl.BlockSpec(memory_space=pltpu.SMEM)
    return pl.pallas_call(
        functools.partial(plan_kernel, blocks),
        out_shape=[
            jax.ShapeDtypeStruct((2 + PEERS + blocks,), jnp.int32),
            jax.ShapeDtypeStruct((1,), jnp.int32),
        ],
        in_specs=[smem] * 2,
        out_specs=[smem] * 2,
    )(me, obs_count)


def pack_kernel(nb, base, cols, listed, info, ens, idx, val, rinv, *refs):
    outs, idx_out, val_out, rinv_out, val_all, rinv_all, sems = refs
    slots = idx.shape[1]
    width = nb * cols
    copies = []
    for d in range(PEERS):
        first = info[2 + d] if listed else base + d * nb
        at = pl.multiple_of(first * cols, cols) if listed else first * cols
        copies.append(
            pltpu.make_async_copy(ens.at[:, pl.ds(at, width), :], outs.at[d], sems.at[d])
        )
    for copy in copies:
        copy.start()
    mine = info[2 + info[0]] if listed else base + info[0] * nb
    slot = lax.broadcasted_iota(jnp.int32, (1, slots), 1)
    val_all[...] = val[...].astype(F32)
    rinv_all[...] = rinv[...].astype(F32)
    for q in range(nb):
        row = pl.ds(mine + q, 1)
        idx_out[q : q + 1, :] = idx[row, :]
        val_out[q : q + 1, :] = val_all[row, :]
        used = slot < info[2 + PEERS + mine + q]
        rinv_out[q : q + 1, :] = jnp.where(used, rinv_all[row, :], 0.0)
    for copy in copies:
        copy.wait()


def pack(nb, base, cols, listed, info, ensemble, idx, val, rinv):
    share, _, state = ensemble.shape
    slots = idx.shape[1]
    smem = pl.BlockSpec(memory_space=pltpu.SMEM)
    vmem = pl.BlockSpec(memory_space=pltpu.VMEM)
    hbm = pl.BlockSpec(memory_space=pl.ANY)
    sent, *rows = pl.pallas_call(
        functools.partial(pack_kernel, nb, base, cols, listed),
        out_shape=[
            jax.ShapeDtypeStruct((PEERS, share, nb * cols, state), BF16),
            jax.ShapeDtypeStruct((nb, slots), jnp.int32),
            jax.ShapeDtypeStruct((nb, slots), F32),
            jax.ShapeDtypeStruct((nb, slots), F32),
        ],
        in_specs=[smem, hbm, vmem, vmem, vmem],
        out_specs=[vmem] * 4,
        scratch_shapes=[
            pltpu.VMEM(val.shape, F32),
            pltpu.VMEM(rinv.shape, F32),
            pltpu.SemaphoreType.DMA((PEERS,)),
        ],
        compiler_params=pltpu.CompilerParams(vmem_limit_bytes=16 * 1024 * 1024),
    )(info, ensemble, idx, val, rinv)
    return sent, rows


def all_kernel(*refs):
    chunks, out, sems = refs[:-2], refs[-2], refs[-1]
    copies = []
    for i, chunk in enumerate(chunks):
        width = chunk.shape[2]
        for d in range(PEERS):
            at = (i * PEERS + d) * width
            copies.append(
                pltpu.make_async_copy(
                    chunk.at[d], out.at[:, pl.ds(at, width), :], sems.at[i * PEERS + d]
                )
            )
    for copy in copies:
        copy.start()
    for copy in copies:
        copy.wait()


def some_kernel(info, ens, chunks, out, sems):
    cols = chunks.shape[2]
    blocks = out.shape[1] // cols
    copies = []
    for b in range(blocks):
        at = b * cols
        copies.append((
            info[2 + PEERS + b] <= 0,
            pltpu.make_async_copy(
                ens.at[:, pl.ds(at, cols), :], out.at[:, pl.ds(at, cols), :], sems.at[b]
            ),
        ))
    for d in range(PEERS):
        at = pl.multiple_of(info[2 + d] * cols, cols)
        copies.append((
            d < info[1],
            pltpu.make_async_copy(
                chunks.at[d], out.at[:, pl.ds(at, cols), :], sems.at[blocks + d]
            ),
        ))
    for wanted, copy in copies:
        pl.when(wanted)(copy.start)
    for wanted, copy in copies:
        pl.when(wanted)(copy.wait)


def assemble(kernel, plans, arrays, chunks, shape, sems):
    hbm = pl.BlockSpec(memory_space=pl.ANY)
    vmem = pl.BlockSpec(memory_space=pltpu.VMEM)
    return pl.pallas_call(
        kernel,
        out_shape=jax.ShapeDtypeStruct(shape, BF16),
        in_specs=[pl.BlockSpec(memory_space=pltpu.SMEM)] * len(plans)
        + [hbm] * len(arrays)
        + [vmem] * len(chunks),
        out_specs=hbm,
        scratch_shapes=[pltpu.SemaphoreType.DMA((sems,))],
        compiler_params=pltpu.CompilerParams(vmem_limit_bytes=16 * 1024 * 1024),
    )(*plans, *arrays, *chunks)


def shards(ensemble, obs_count, obs_index, obs_value, obs_rinv):
    share, columns, state = ensemble.shape
    blocks = obs_count.shape[0]
    cols = columns // blocks
    me = lax.axis_index("mem").astype(jnp.int32)
    info, load = make_plan(me[None], obs_count)

    def exchange(x):
        return lax.all_to_all(x, "mem", 0, 0, tiled=True)

    def run(nb, base, listed):
        sent, rows = pack(
            nb, base, cols, listed, info, ensemble, obs_index, obs_value, obs_rinv
        )
        return exchange(analyse(nb, cols, *rows, exchange(sent)))

    def whole():
        step = blocks // PARTS
        back = [run(step // PEERS, i * step, False) for i in range(PARTS)]
        return assemble(all_kernel, [], [], back, ensemble.shape, PEERS * PARTS)

    def part():
        back = run(1, 0, True)
        return assemble(
            some_kernel, [info], [ensemble], [back], ensemble.shape, blocks + PEERS
        )

    return lax.cond(load[0] > PEERS, whole, part)


def solution(mesh):
    return jax.shard_map(
        shards,
        mesh=mesh,
        in_specs=(
            P("mem", "space", None),
            P("space"),
            P("space", None),
            P("space", None),
            P("space", None),
        ),
        out_specs=P("mem", "space", None),
        check_vma=False,
    )
```

```python
import functools
import math

import jax
import jax.numpy as jnp
from jax import lax
from jax.experimental import pallas as pl
from jax.experimental.pallas import tpu as pltpu
from jax.sharding import PartitionSpec as P

SWEEPS = 8
F32 = jnp.float32
BF16 = jnp.bfloat16


def split(x):
    high = x.astype(BF16)
    low = (x - high.astype(F32)).astype(BF16)
    return high, low


def as_left(pieces):
    return jnp.concatenate([jnp.concatenate([h, l], axis=1) for h, l in pieces], axis=0)


def as_right(piece):
    row = jnp.concatenate(piece, axis=1)
    return jnp.concatenate([row, row], axis=0)


def product(left, right):
    full = jnp.dot(left, right, preferred_element_type=F32)
    half = full.shape[1] // 2
    return full[:, :half] + full[:, half:]


def analyse_kernel(nb, cols, idx_ref, val_ref, rinv_ref, chunks, outs, both_ref):
    share = chunks.shape[1]
    members = share * PEERS
    state = chunks.shape[3]
    slots = idx_ref.shape[1]
    tall = share * cols
    row_iota = lax.broadcasted_iota(jnp.int32, (members, members), 0)
    col_iota = lax.broadcasted_iota(jnp.int32, (members, members), 1)
    identity = (row_iota == col_iota).astype(F32)
    tall_row = lax.broadcasted_iota(jnp.int32, (tall, tall), 0)
    tall_col = lax.broadcasted_iota(jnp.int32, (tall, tall), 1)
    swap = (tall_col == (tall_row % share) * cols + tall_row // share).astype(F32).astype(BF16)
    ones = jnp.ones((16, members), BF16)
    zs = []
    for q in range(nb):
        for d in range(0, PEERS, 2):
            pair = jnp.concatenate(
                [
                    chunks[e, :, q * cols : (q + 1) * cols, :].reshape(tall, state)
                    for e in (d, d + 1)
                ],
                axis=1,
            )
            turned = jnp.dot(swap, pair, preferred_element_type=F32).astype(BF16)
            for e in (0, 1):
                for c in range(cols):
                    both_ref[
                        q, (d + e) * share : (d + e + 1) * share, c * state : (c + 1) * state
                    ] = turned[c * share : (c + 1) * share, e * state : (e + 1) * state]
    for q in range(nb):
        raw = both_ref[q, :members]
        mean = jnp.dot(ones, raw, preferred_element_type=F32) / members
        high, low = split(mean)
        rest = (mean - high.astype(F32) - low.astype(F32)).astype(BF16)
        turn = lax.broadcasted_iota(jnp.int32, mean.shape, 0) % 3
        pick = lambda p: p.astype(F32)
        both_ref[q, members:] = jnp.where(
            turn == 0, pick(high), jnp.where(turn == 1, pick(low), pick(rest))
        ).astype(BF16)
    tables = []
    for q in range(nb):
        idx = idx_ref[q : q + 1, :]
        spot_col = idx // state
        spot_state = idx - spot_col * state
        state_hit = (
            lax.broadcasted_iota(jnp.int32, (state, slots), 0) == spot_state
        ).astype(F32).astype(BF16)
        tables.append(
            jnp.concatenate(
                [state_hit * (spot_col == c).astype(F32).astype(BF16) for c in range(cols)],
                axis=0,
            )
        )
    spots = [
        jnp.dot(both_ref[q, :members], tables[q], preferred_element_type=F32)
        for q in range(nb)
    ]
    spot_means = [jnp.sum(x, axis=0, keepdims=True) / members for x in spots]
    obs_perts = [(x - m).astype(BF16) for x, m in zip(spots, spot_means)]
    gathered = []
    for q in range(nb):
        innov = (val_ref[q : q + 1, :] - spot_means[q]).astype(BF16)
        weighted = (obs_perts[q].astype(F32) * rinv_ref[q : q + 1, :]).astype(BF16)
        left = jnp.concatenate([obs_perts[q], jnp.broadcast_to(innov, (16, slots))], axis=0)
        gathered.append(
            lax.dot_general(
                left, weighted, (((1,), (1,)), ((), ())), preferred_element_type=F32
            )
        )
    grams = [x[:members] + (members - 1.0) * identity for x in gathered]
    scales = [
        jnp.sum(jnp.sum(g * identity, axis=0, keepdims=True), axis=1, keepdims=True)
        for g in grams
    ]
    ws = [g / scale for g, scale in zip(grams, scales)]
    us = [x[members:] for x in gathered]
    pieces = [split(w) for w in ws]
    rights = [as_right(p) for p in pieces]
    firsts = [product(as_left([pieces[q], split(us[q])]), rights[q]) for q in range(nb)]
    seconds = [product(as_left([split(firsts[q])]), rights[q]) for q in range(nb)]
    for q in range(nb):
        w, u, first, second = ws[q], us[q], firsts[q], seconds[q]
        zs.append(1.5 * identity - 0.5 * w)
        ws[q] = 2.25 * w - 1.5 * first[:members] + 0.25 * second[:members]
        us[q] = 2.25 * u - 1.5 * first[members:] + 0.25 * second[members:]
    for sweep in range(1, SWEEPS - 1):
        pieces = [split(w) for w in ws]
        rights = [as_right(p) for p in pieces]
        firsts = [
            product(as_left([pieces[q], split(us[q])]), rights[q]) for q in range(nb)
        ]
        seconds = [product(as_left([split(firsts[q])]), rights[q]) for q in range(nb)]
        for q in range(nb):
            zw = product(as_left([split(zs[q])]), rights[q])
            zs[q] = 1.5 * zs[q] - 0.5 * zw
        for q in range(nb):
            w, u, first, second = ws[q], us[q], firsts[q], seconds[q]
            ws[q] = 2.25 * w - 1.5 * first[:members] + 0.25 * second[:members]
            us[q] = 2.25 * u - 1.5 * first[members:] + 0.25 * second[members:]
    rights = [as_right(split(w)) for w in ws]
    firsts = [product(as_left([split(zs[q]), split(us[q])]), rights[q]) for q in range(nb)]
    seconds = [product(as_left([split(firsts[q][members:])]), rights[q]) for q in range(nb)]
    lefts = []
    for q in range(nb):
        z = 1.5 * zs[q] - 0.5 * firsts[q][:members]
        u = 2.25 * us[q] - 1.5 * firsts[q][members:] + 0.25 * seconds[q]
        scale = scales[q]
        weights = ((math.sqrt(members - 1.0) / jnp.sqrt(scale)) * z + u[:1] / scale).astype(BF16)
        spare = 1.0 - jnp.sum(weights.astype(F32), axis=1, keepdims=True)
        high, low = split(spare)
        lane = lax.broadcasted_iota(jnp.int32, (members, 16), 1)
        tail = jnp.where(
            lane < 3, high.astype(F32), jnp.where(lane < 6, low.astype(F32), 0.0)
        ).astype(BF16)
        lefts.append(jnp.concatenate([weights, tail], axis=1))
    for q in range(nb):
        result = jnp.dot(lefts[q], both_ref[q], preferred_element_type=F32).astype(BF16)
        for d in range(0, PEERS, 2):
            pair = jnp.concatenate(
                [
                    jnp.concatenate(
                        [
                            result[e * share : (e + 1) * share, c * state : (c + 1) * state]
                            for c in range(cols)
                        ],
                        axis=0,
                    )
                    for e in (d, d + 1)
                ],
                axis=1,
            )
            turned = jnp.dot(swap, pair, preferred_element_type=F32).astype(BF16)
            for e in (0, 1):
                outs[d + e, :, q * cols : (q + 1) * cols, :] = turned[
                    :, e * state : (e + 1) * state
                ].reshape(share, cols, state)


def analyse(nb, cols, idx, val, rinv, chunks):
    peers, share, _, state = chunks.shape
    members = share * peers
    vmem = pl.BlockSpec(memory_space=pltpu.VMEM)
    return pl.pallas_call(
        functools.partial(analyse_kernel, nb, cols),
        out_shape=jax.ShapeDtypeStruct(chunks.shape, chunks.dtype),
        in_specs=[vmem] * 4,
        out_specs=vmem,
        scratch_shapes=[pltpu.VMEM((nb, members + 16, cols * state), BF16)],
        compiler_params=pltpu.CompilerParams(vmem_limit_bytes=24 * 1024 * 1024),
        cost_estimate=pl.CostEstimate(
            flops=nb * 2_000_000_000, bytes_accessed=nb * 1_048_576, transcendentals=0
        ),
    )(idx, val, rinv, chunks)


PEERS = 8


def plan_kernel(blocks, me, count, info, load):
    turn = jnp.int32(0)
    for r in range(PEERS):
        info[2 + r] = 0
    for b in range(blocks):
        seen = count[b]
        info[2 + PEERS + b] = seen

        @pl.when((seen > 0) & (turn < PEERS))
        def _():
            info[2 + turn] = b

        turn = turn + (seen > 0).astype(jnp.int32)
    info[0] = me[0]
    info[1] = turn
    load[0] = turn


def make_plan(me, obs_count):
    blocks = obs_count.shape[0]
    smem = pl.BlockSpec(memory_space=pltpu.SMEM)
    return pl.pallas_call(
        functools.partial(plan_kernel, blocks),
        out_shape=[
            jax.ShapeDtypeStruct((2 + PEERS + blocks,), jnp.int32),
            jax.ShapeDtypeStruct((1,), jnp.int32),
        ],
        in_specs=[smem] * 2,
        out_specs=[smem] * 2,
    )(me, obs_count)


def pack_kernel(nb, base, cols, listed, info, ens, idx, val, rinv, *refs):
    outs, idx_out, val_out, rinv_out, val_all, rinv_all, sems = refs
    slots = idx.shape[1]
    width = nb * cols
    copies = []
    for d in range(PEERS):
        first = info[2 + d] if listed else base + d * nb
        at = pl.multiple_of(first * cols, cols) if listed else first * cols
        copies.append(
            pltpu.make_async_copy(ens.at[:, pl.ds(at, width), :], outs.at[d], sems.at[d])
        )
    for copy in copies:
        copy.start()
    mine = info[2 + info[0]] if listed else base + info[0] * nb
    slot = lax.broadcasted_iota(jnp.int32, (1, slots), 1)
    val_all[...] = val[...].astype(F32)
    rinv_all[...] = rinv[...].astype(F32)
    for q in range(nb):
        row = pl.ds(mine + q, 1)
        idx_out[q : q + 1, :] = idx[row, :]
        val_out[q : q + 1, :] = val_all[row, :]
        used = slot < info[2 + PEERS + mine + q]
        rinv_out[q : q + 1, :] = jnp.where(used, rinv_all[row, :], 0.0)
    for copy in copies:
        copy.wait()


def pack(nb, base, cols, listed, info, ensemble, idx, val, rinv):
    share, _, state = ensemble.shape
    slots = idx.shape[1]
    smem = pl.BlockSpec(memory_space=pltpu.SMEM)
    vmem = pl.BlockSpec(memory_space=pltpu.VMEM)
    hbm = pl.BlockSpec(memory_space=pl.ANY)
    sent, *rows = pl.pallas_call(
        functools.partial(pack_kernel, nb, base, cols, listed),
        out_shape=[
            jax.ShapeDtypeStruct((PEERS, share, nb * cols, state), BF16),
            jax.ShapeDtypeStruct((nb, slots), jnp.int32),
            jax.ShapeDtypeStruct((nb, slots), F32),
            jax.ShapeDtypeStruct((nb, slots), F32),
        ],
        in_specs=[smem, hbm, vmem, vmem, vmem],
        out_specs=[vmem] * 4,
        scratch_shapes=[
            pltpu.VMEM(val.shape, F32),
            pltpu.VMEM(rinv.shape, F32),
            pltpu.SemaphoreType.DMA((PEERS,)),
        ],
        compiler_params=pltpu.CompilerParams(vmem_limit_bytes=16 * 1024 * 1024),
    )(info, ensemble, idx, val, rinv)
    return sent, rows


def all_kernel(*refs):
    chunks, out, sems = refs[:-2], refs[-2], refs[-1]
    copies = []
    for i, chunk in enumerate(chunks):
        width = chunk.shape[2]
        for d in range(PEERS):
            at = (i * PEERS + d) * width
            copies.append(
                pltpu.make_async_copy(
                    chunk.at[d], out.at[:, pl.ds(at, width), :], sems.at[i * PEERS + d]
                )
            )
    for copy in copies:
        copy.start()
    for copy in copies:
        copy.wait()


def some_kernel(info, ens, chunks, out, sems):
    cols = chunks.shape[2]
    blocks = out.shape[1] // cols
    copies = []
    for b in range(blocks):
        at = b * cols
        copies.append((
            info[2 + PEERS + b] <= 0,
            pltpu.make_async_copy(
                ens.at[:, pl.ds(at, cols), :], out.at[:, pl.ds(at, cols), :], sems.at[b]
            ),
        ))
    for d in range(PEERS):
        at = pl.multiple_of(info[2 + d] * cols, cols)
        copies.append((
            d < info[1],
            pltpu.make_async_copy(
                chunks.at[d], out.at[:, pl.ds(at, cols), :], sems.at[blocks + d]
            ),
        ))
    for wanted, copy in copies:
        pl.when(wanted)(copy.start)
    for wanted, copy in copies:
        pl.when(wanted)(copy.wait)


def assemble(kernel, plans, arrays, chunks, shape, sems):
    hbm = pl.BlockSpec(memory_space=pl.ANY)
    vmem = pl.BlockSpec(memory_space=pltpu.VMEM)
    return pl.pallas_call(
        kernel,
        out_shape=jax.ShapeDtypeStruct(shape, BF16),
        in_specs=[pl.BlockSpec(memory_space=pltpu.SMEM)] * len(plans)
        + [hbm] * len(arrays)
        + [vmem] * len(chunks),
        out_specs=hbm,
        scratch_shapes=[pltpu.SemaphoreType.DMA((sems,))],
        compiler_params=pltpu.CompilerParams(vmem_limit_bytes=16 * 1024 * 1024),
    )(*plans, *arrays, *chunks)


def shards(ensemble, obs_count, obs_index, obs_value, obs_rinv):
    share, columns, state = ensemble.shape
    blocks = obs_count.shape[0]
    cols = columns // blocks
    me = lax.axis_index("mem").astype(jnp.int32)
    info, load = make_plan(me[None], obs_count)

    def exchange(x):
        return lax.all_to_all(x, "mem", 0, 0, tiled=True)

    def run(nb, base, listed):
        sent, rows = pack(
            nb, base, cols, listed, info, ensemble, obs_index, obs_value, obs_rinv
        )
        return exchange(analyse(nb, cols, *rows, exchange(sent)))

    def whole():
        back = run(blocks // PEERS, 0, False)
        return assemble(all_kernel, [], [], [back], ensemble.shape, PEERS)

    def part():
        back = run(1, 0, True)
        return assemble(
            some_kernel, [info], [ensemble], [back], ensemble.shape, blocks + PEERS
        )

    return lax.cond(load[0] > PEERS, whole, part)


def solution(mesh):
    return jax.shard_map(
        shards,
        mesh=mesh,
        in_specs=(
            P("mem", "space", None),
            P("space"),
            P("space", None),
            P("space", None),
            P("space", None),
        ),
        out_specs=P("mem", "space", None),
        check_vma=False,
    )
```

```python
import functools
import math

import jax
import jax.numpy as jnp
from jax import lax
from jax.experimental import pallas as pl
from jax.experimental.pallas import tpu as pltpu
from jax.sharding import PartitionSpec as P

SWEEPS = 8
F32 = jnp.float32
BF16 = jnp.bfloat16


def split(x):
    high = x.astype(BF16)
    low = (x - high.astype(F32)).astype(BF16)
    return high, low


def as_left(pieces):
    return jnp.concatenate([jnp.concatenate([h, l], axis=1) for h, l in pieces], axis=0)


def as_right(piece):
    row = jnp.concatenate(piece, axis=1)
    return jnp.concatenate([row, row], axis=0)


def product(left, right):
    full = jnp.dot(left, right, preferred_element_type=F32)
    half = full.shape[1] // 2
    return full[:, :half] + full[:, half:]


def analyse_kernel(nb, cols, idx_ref, val_ref, rinv_ref, chunks, outs, both_ref):
    share = chunks.shape[1]
    members = share * PEERS
    state = chunks.shape[3]
    slots = idx_ref.shape[1]
    tall = share * cols
    row_iota = lax.broadcasted_iota(jnp.int32, (members, members), 0)
    col_iota = lax.broadcasted_iota(jnp.int32, (members, members), 1)
    identity = (row_iota == col_iota).astype(F32)
    tall_row = lax.broadcasted_iota(jnp.int32, (tall, tall), 0)
    tall_col = lax.broadcasted_iota(jnp.int32, (tall, tall), 1)
    swap = (tall_col == (tall_row % share) * cols + tall_row // share).astype(F32).astype(BF16)
    zs = []
    for q in range(nb):
        for d in range(0, PEERS, 2):
            pair = jnp.concatenate(
                [
                    chunks[e, :, q * cols : (q + 1) * cols, :].reshape(tall, state)
                    for e in (d, d + 1)
                ],
                axis=1,
            )
            turned = jnp.dot(swap, pair, preferred_element_type=F32).astype(BF16)
            for e in (0, 1):
                for c in range(cols):
                    both_ref[
                        q, (d + e) * share : (d + e + 1) * share, c * state : (c + 1) * state
                    ] = turned[c * share : (c + 1) * share, e * state : (e + 1) * state]
    tables = []
    for q in range(nb):
        idx = idx_ref[q : q + 1, :]
        spot_col = idx // state
        spot_state = idx - spot_col * state
        state_hit = (
            lax.broadcasted_iota(jnp.int32, (state, slots), 0) == spot_state
        ).astype(F32).astype(BF16)
        tables.append(
            jnp.concatenate(
                [state_hit * (spot_col == c).astype(F32).astype(BF16) for c in range(cols)],
                axis=0,
            )
        )
    spots = [
        jnp.dot(both_ref[q, :members], tables[q], preferred_element_type=F32)
        for q in range(nb)
    ]
    spot_means = [jnp.sum(x, axis=0, keepdims=True) / members for x in spots]
    obs_perts = [(x - m).astype(BF16) for x, m in zip(spots, spot_means)]
    gathered = []
    for q in range(nb):
        innov = (val_ref[q : q + 1, :] - spot_means[q]).astype(BF16)
        weighted = (obs_perts[q].astype(F32) * rinv_ref[q : q + 1, :]).astype(BF16)
        left = jnp.concatenate([obs_perts[q], jnp.broadcast_to(innov, (16, slots))], axis=0)
        gathered.append(
            lax.dot_general(
                left, weighted, (((1,), (1,)), ((), ())), preferred_element_type=F32
            )
        )
    grams = [x[:members] + (members - 1.0) * identity for x in gathered]
    scales = [
        jnp.sum(jnp.sum(g * identity, axis=0, keepdims=True), axis=1, keepdims=True)
        for g in grams
    ]
    ws = [g / scale for g, scale in zip(grams, scales)]
    us = [x[members:] for x in gathered]
    pieces = [split(w) for w in ws]
    rights = [as_right(p) for p in pieces]
    firsts = [product(as_left([pieces[q], split(us[q])]), rights[q]) for q in range(nb)]
    seconds = [product(as_left([split(firsts[q])]), rights[q]) for q in range(nb)]
    for q in range(nb):
        w, u, first, second = ws[q], us[q], firsts[q], seconds[q]
        zs.append(1.5 * identity - 0.5 * w)
        ws[q] = 2.25 * w - 1.5 * first[:members] + 0.25 * second[:members]
        us[q] = 2.25 * u - 1.5 * first[members:] + 0.25 * second[members:]
    for sweep in range(1, SWEEPS - 1):
        pieces = [split(w) for w in ws]
        rights = [as_right(p) for p in pieces]
        firsts = [
            product(as_left([pieces[q], split(us[q])]), rights[q]) for q in range(nb)
        ]
        seconds = [product(as_left([split(firsts[q])]), rights[q]) for q in range(nb)]
        for q in range(nb):
            zw = product(as_left([split(zs[q])]), rights[q])
            zs[q] = 1.5 * zs[q] - 0.5 * zw
        for q in range(nb):
            w, u, first, second = ws[q], us[q], firsts[q], seconds[q]
            ws[q] = 2.25 * w - 1.5 * first[:members] + 0.25 * second[:members]
            us[q] = 2.25 * u - 1.5 * first[members:] + 0.25 * second[members:]
    rights = [as_right(split(w)) for w in ws]
    firsts = [product(as_left([split(zs[q]), split(us[q])]), rights[q]) for q in range(nb)]
    seconds = [product(as_left([split(firsts[q][members:])]), rights[q]) for q in range(nb)]
    lefts = []
    for q in range(nb):
        z = 1.5 * zs[q] - 0.5 * firsts[q][:members]
        u = 2.25 * us[q] - 1.5 * firsts[q][members:] + 0.25 * seconds[q]
        scale = scales[q]
        weights = (math.sqrt(members - 1.0) / jnp.sqrt(scale)) * z + u[:1] / scale
        spare = (1.0 - jnp.sum(weights, axis=1, keepdims=True)) / members
        lefts.append(jnp.concatenate(split(weights + spare), axis=1))
    results = []
    for q in range(nb):
        raw = both_ref[q]
        results.append(
            jnp.dot(
                lefts[q], jnp.concatenate([raw, raw], axis=0), preferred_element_type=F32
            ).astype(BF16)
        )
    for q, result in enumerate(results):
        for d in range(0, PEERS, 2):
            pair = jnp.concatenate(
                [
                    jnp.concatenate(
                        [
                            result[e * share : (e + 1) * share, c * state : (c + 1) * state]
                            for c in range(cols)
                        ],
                        axis=0,
                    )
                    for e in (d, d + 1)
                ],
                axis=1,
            )
            turned = jnp.dot(swap, pair, preferred_element_type=F32).astype(BF16)
            for e in (0, 1):
                outs[d + e, :, q * cols : (q + 1) * cols, :] = turned[
                    :, e * state : (e + 1) * state
                ].reshape(share, cols, state)


def analyse(nb, cols, idx, val, rinv, chunks):
    peers, share, _, state = chunks.shape
    members = share * peers
    vmem = pl.BlockSpec(memory_space=pltpu.VMEM)
    return pl.pallas_call(
        functools.partial(analyse_kernel, nb, cols),
        out_shape=jax.ShapeDtypeStruct(chunks.shape, chunks.dtype),
        in_specs=[vmem] * 4,
        out_specs=vmem,
        scratch_shapes=[pltpu.VMEM((nb, members, cols * state), BF16)],
        compiler_params=pltpu.CompilerParams(vmem_limit_bytes=24 * 1024 * 1024),
        cost_estimate=pl.CostEstimate(
            flops=nb * 2_000_000_000, bytes_accessed=nb * 1_048_576, transcendentals=0
        ),
    )(idx, val, rinv, chunks)


PEERS = 8


def plan_kernel(blocks, me, count, info, load):
    turn = jnp.int32(0)
    for r in range(PEERS):
        info[2 + r] = 0
    for b in range(blocks):
        seen = count[b]
        info[2 + PEERS + b] = seen

        @pl.when((seen > 0) & (turn < PEERS))
        def _():
            info[2 + turn] = b

        turn = turn + (seen > 0).astype(jnp.int32)
    info[0] = me[0]
    info[1] = turn
    load[0] = turn


def make_plan(me, obs_count):
    blocks = obs_count.shape[0]
    smem = pl.BlockSpec(memory_space=pltpu.SMEM)
    return pl.pallas_call(
        functools.partial(plan_kernel, blocks),
        out_shape=[
            jax.ShapeDtypeStruct((2 + PEERS + blocks,), jnp.int32),
            jax.ShapeDtypeStruct((1,), jnp.int32),
        ],
        in_specs=[smem] * 2,
        out_specs=[smem] * 2,
    )(me, obs_count)


def pack_kernel(nb, base, cols, listed, info, ens, idx, val, rinv, *refs):
    outs, idx_out, val_out, rinv_out, val_all, rinv_all, sems = refs
    slots = idx.shape[1]
    width = nb * cols
    copies = []
    for d in range(PEERS):
        first = info[2 + d] if listed else base + d * nb
        at = pl.multiple_of(first * cols, cols) if listed else first * cols
        copies.append(
            pltpu.make_async_copy(ens.at[:, pl.ds(at, width), :], outs.at[d], sems.at[d])
        )
    for copy in copies:
        copy.start()
    mine = info[2 + info[0]] if listed else base + info[0] * nb
    slot = lax.broadcasted_iota(jnp.int32, (1, slots), 1)
    val_all[...] = val[...].astype(F32)
    rinv_all[...] = rinv[...].astype(F32)
    for q in range(nb):
        row = pl.ds(mine + q, 1)
        idx_out[q : q + 1, :] = idx[row, :]
        val_out[q : q + 1, :] = val_all[row, :]
        used = slot < info[2 + PEERS + mine + q]
        rinv_out[q : q + 1, :] = jnp.where(used, rinv_all[row, :], 0.0)
    for copy in copies:
        copy.wait()


def pack(nb, base, cols, listed, info, ensemble, idx, val, rinv):
    share, _, state = ensemble.shape
    slots = idx.shape[1]
    smem = pl.BlockSpec(memory_space=pltpu.SMEM)
    vmem = pl.BlockSpec(memory_space=pltpu.VMEM)
    hbm = pl.BlockSpec(memory_space=pl.ANY)
    sent, *rows = pl.pallas_call(
        functools.partial(pack_kernel, nb, base, cols, listed),
        out_shape=[
            jax.ShapeDtypeStruct((PEERS, share, nb * cols, state), BF16),
            jax.ShapeDtypeStruct((nb, slots), jnp.int32),
            jax.ShapeDtypeStruct((nb, slots), F32),
            jax.ShapeDtypeStruct((nb, slots), F32),
        ],
        in_specs=[smem, hbm, vmem, vmem, vmem],
        out_specs=[vmem] * 4,
        scratch_shapes=[
            pltpu.VMEM(val.shape, F32),
            pltpu.VMEM(rinv.shape, F32),
            pltpu.SemaphoreType.DMA((PEERS,)),
        ],
        compiler_params=pltpu.CompilerParams(vmem_limit_bytes=16 * 1024 * 1024),
    )(info, ensemble, idx, val, rinv)
    return sent, rows


def all_kernel(*refs):
    chunks, out, sems = refs[:-2], refs[-2], refs[-1]
    copies = []
    for i, chunk in enumerate(chunks):
        width = chunk.shape[2]
        for d in range(PEERS):
            at = (i * PEERS + d) * width
            copies.append(
                pltpu.make_async_copy(
                    chunk.at[d], out.at[:, pl.ds(at, width), :], sems.at[i * PEERS + d]
                )
            )
    for copy in copies:
        copy.start()
    for copy in copies:
        copy.wait()


def some_kernel(info, ens, chunks, out, sems):
    cols = chunks.shape[2]
    blocks = out.shape[1] // cols
    copies = []
    for b in range(blocks):
        at = b * cols
        copies.append((
            info[2 + PEERS + b] <= 0,
            pltpu.make_async_copy(
                ens.at[:, pl.ds(at, cols), :], out.at[:, pl.ds(at, cols), :], sems.at[b]
            ),
        ))
    for d in range(PEERS):
        at = pl.multiple_of(info[2 + d] * cols, cols)
        copies.append((
            d < info[1],
            pltpu.make_async_copy(
                chunks.at[d], out.at[:, pl.ds(at, cols), :], sems.at[blocks + d]
            ),
        ))
    for wanted, copy in copies:
        pl.when(wanted)(copy.start)
    for wanted, copy in copies:
        pl.when(wanted)(copy.wait)


def assemble(kernel, plans, arrays, chunks, shape, sems):
    hbm = pl.BlockSpec(memory_space=pl.ANY)
    vmem = pl.BlockSpec(memory_space=pltpu.VMEM)
    return pl.pallas_call(
        kernel,
        out_shape=jax.ShapeDtypeStruct(shape, BF16),
        in_specs=[pl.BlockSpec(memory_space=pltpu.SMEM)] * len(plans)
        + [hbm] * len(arrays)
        + [vmem] * len(chunks),
        out_specs=hbm,
        scratch_shapes=[pltpu.SemaphoreType.DMA((sems,))],
        compiler_params=pltpu.CompilerParams(vmem_limit_bytes=16 * 1024 * 1024),
    )(*plans, *arrays, *chunks)


def shards(ensemble, obs_count, obs_index, obs_value, obs_rinv):
    share, columns, state = ensemble.shape
    blocks = obs_count.shape[0]
    cols = columns // blocks
    me = lax.axis_index("mem").astype(jnp.int32)
    info, load = make_plan(me[None], obs_count)

    def exchange(x):
        return lax.all_to_all(x, "mem", 0, 0, tiled=True)

    def run(nb, base, listed):
        sent, rows = pack(
            nb, base, cols, listed, info, ensemble, obs_index, obs_value, obs_rinv
        )
        return exchange(analyse(nb, cols, *rows, exchange(sent)))

    def whole():
        back = run(blocks // PEERS, 0, False)
        return assemble(all_kernel, [], [], [back], ensemble.shape, PEERS)

    def part():
        back = run(1, 0, True)
        return assemble(
            some_kernel, [info], [ensemble], [back], ensemble.shape, blocks + PEERS
        )

    return lax.cond(load[0] > PEERS, whole, part)


def solution(mesh):
    return jax.shard_map(
        shards,
        mesh=mesh,
        in_specs=(
            P("mem", "space", None),
            P("space"),
            P("space", None),
            P("space", None),
            P("space", None),
        ),
        out_specs=P("mem", "space", None),
        check_vma=False,
    )
```

```python
import functools
import math

import jax
import jax.numpy as jnp
from jax import lax
from jax.experimental import pallas as pl
from jax.experimental.pallas import tpu as pltpu
from jax.sharding import PartitionSpec as P

SWEEPS = 8
F32 = jnp.float32
BF16 = jnp.bfloat16


def split(x):
    high = x.astype(BF16)
    low = (x - high.astype(F32)).astype(BF16)
    return high, low


def as_left(pieces):
    return jnp.concatenate([jnp.concatenate([h, l], axis=1) for h, l in pieces], axis=0)


def as_right(piece):
    row = jnp.concatenate(piece, axis=1)
    return jnp.concatenate([row, row], axis=0)


def product(left, right):
    full = jnp.dot(left, right, preferred_element_type=F32)
    half = full.shape[1] // 2
    return full[:, :half] + full[:, half:]


def analyse_kernel(nb, cols, idx_ref, val_ref, rinv_ref, chunks, outs, both_ref):
    share = chunks.shape[1]
    members = share * PEERS
    state = chunks.shape[3]
    slots = idx_ref.shape[1]
    tall = share * cols
    row_iota = lax.broadcasted_iota(jnp.int32, (members, members), 0)
    col_iota = lax.broadcasted_iota(jnp.int32, (members, members), 1)
    identity = (row_iota == col_iota).astype(F32)
    tall_row = lax.broadcasted_iota(jnp.int32, (tall, tall), 0)
    tall_col = lax.broadcasted_iota(jnp.int32, (tall, tall), 1)
    swap = (tall_col == (tall_row % share) * cols + tall_row // share).astype(F32).astype(BF16)
    zs = []
    for q in range(nb):
        for d in range(0, PEERS, 2):
            pair = jnp.concatenate(
                [
                    chunks[e, :, q * cols : (q + 1) * cols, :].reshape(tall, state)
                    for e in (d, d + 1)
                ],
                axis=1,
            )
            turned = jnp.dot(swap, pair, preferred_element_type=F32).astype(BF16)
            for e in (0, 1):
                for c in range(cols):
                    both_ref[
                        q, (d + e) * share : (d + e + 1) * share, c * state : (c + 1) * state
                    ] = turned[c * share : (c + 1) * share, e * state : (e + 1) * state]
    tables = []
    for q in range(nb):
        idx = idx_ref[q : q + 1, :]
        spot_col = idx // state
        spot_state = idx - spot_col * state
        state_hit = (
            lax.broadcasted_iota(jnp.int32, (state, slots), 0) == spot_state
        ).astype(F32).astype(BF16)
        tables.append(
            jnp.concatenate(
                [state_hit * (spot_col == c).astype(F32).astype(BF16) for c in range(cols)],
                axis=0,
            )
        )
    spots = [
        jnp.dot(both_ref[q, :members], tables[q], preferred_element_type=F32)
        for q in range(nb)
    ]
    spot_means = [jnp.sum(x, axis=0, keepdims=True) / members for x in spots]
    obs_perts = [(x - m).astype(BF16) for x, m in zip(spots, spot_means)]
    gathered = []
    for q in range(nb):
        innov = (val_ref[q : q + 1, :] - spot_means[q]).astype(BF16)
        weighted = (obs_perts[q].astype(F32) * rinv_ref[q : q + 1, :]).astype(BF16)
        left = jnp.concatenate([obs_perts[q], jnp.broadcast_to(innov, (16, slots))], axis=0)
        gathered.append(
            lax.dot_general(
                left, weighted, (((1,), (1,)), ((), ())), preferred_element_type=F32
            )
        )
    grams = [x[:members] + (members - 1.0) * identity for x in gathered]
    scales = [
        jnp.sum(jnp.sum(g * identity, axis=0, keepdims=True), axis=1, keepdims=True)
        for g in grams
    ]
    ws = [g / scale for g, scale in zip(grams, scales)]
    us = [x[members:] for x in gathered]
    pieces = [split(w) for w in ws]
    rights = [as_right(p) for p in pieces]
    firsts = [product(as_left([pieces[q], split(us[q])]), rights[q]) for q in range(nb)]
    seconds = [product(as_left([split(firsts[q])]), rights[q]) for q in range(nb)]
    for q in range(nb):
        w, u, first, second = ws[q], us[q], firsts[q], seconds[q]
        zs.append(1.5 * identity - 0.5 * w)
        ws[q] = 2.25 * w - 1.5 * first[:members] + 0.25 * second[:members]
        us[q] = 2.25 * u - 1.5 * first[members:] + 0.25 * second[members:]
    for sweep in range(1, SWEEPS - 1):
        pieces = [split(w) for w in ws]
        rights = [as_right(p) for p in pieces]
        firsts = [
            product(as_left([pieces[q], split(us[q])]), rights[q]) for q in range(nb)
        ]
        seconds = [product(as_left([split(firsts[q])]), rights[q]) for q in range(nb)]
        for q in range(nb):
            zw = product(as_left([split(zs[q])]), rights[q])
            zs[q] = 1.5 * zs[q] - 0.5 * zw
        for q in range(nb):
            w, u, first, second = ws[q], us[q], firsts[q], seconds[q]
            ws[q] = 2.25 * w - 1.5 * first[:members] + 0.25 * second[:members]
            us[q] = 2.25 * u - 1.5 * first[members:] + 0.25 * second[members:]
    rights = [as_right(split(w)) for w in ws]
    firsts = [product(as_left([split(zs[q]), split(us[q])]), rights[q]) for q in range(nb)]
    seconds = [product(as_left([split(firsts[q][members:])]), rights[q]) for q in range(nb)]
    lefts = []
    for q in range(nb):
        z = 1.5 * zs[q] - 0.5 * firsts[q][:members]
        u = 2.25 * us[q] - 1.5 * firsts[q][members:] + 0.25 * seconds[q]
        scale = scales[q]
        weights = (math.sqrt(members - 1.0) / jnp.sqrt(scale)) * z + u[:1] / scale
        spare = (1.0 - jnp.sum(weights, axis=1, keepdims=True)) / members
        lefts.append(jnp.concatenate(split(weights + spare), axis=1))
    results = []
    for q in range(nb):
        raw = both_ref[q]
        results.append(
            jnp.dot(
                lefts[q], jnp.concatenate([raw, raw], axis=0), preferred_element_type=F32
            ).astype(BF16)
        )
    for q, result in enumerate(results):
        for d in range(0, PEERS, 2):
            pair = jnp.concatenate(
                [
                    jnp.concatenate(
                        [
                            result[e * share : (e + 1) * share, c * state : (c + 1) * state]
                            for c in range(cols)
                        ],
                        axis=0,
                    )
                    for e in (d, d + 1)
                ],
                axis=1,
            )
            turned = jnp.dot(swap, pair, preferred_element_type=F32).astype(BF16)
            for e in (0, 1):
                outs[d + e, :, q * cols : (q + 1) * cols, :] = turned[
                    :, e * state : (e + 1) * state
                ].reshape(share, cols, state)


def analyse(nb, cols, idx, val, rinv, chunks):
    peers, share, _, state = chunks.shape
    members = share * peers
    vmem = pl.BlockSpec(memory_space=pltpu.VMEM)
    return pl.pallas_call(
        functools.partial(analyse_kernel, nb, cols),
        out_shape=jax.ShapeDtypeStruct(chunks.shape, chunks.dtype),
        in_specs=[vmem] * 4,
        out_specs=vmem,
        scratch_shapes=[pltpu.VMEM((nb, members, cols * state), BF16)],
        compiler_params=pltpu.CompilerParams(vmem_limit_bytes=24 * 1024 * 1024),
        cost_estimate=pl.CostEstimate(
            flops=nb * 2_000_000_000, bytes_accessed=nb * 1_048_576, transcendentals=0
        ),
    )(idx, val, rinv, chunks)


PEERS = 8


def plan_kernel(blocks, me, count, info, load):
    turn = jnp.int32(0)
    for r in range(PEERS):
        info[2 + r] = 0
    for b in range(blocks):
        seen = count[b]
        info[2 + PEERS + b] = seen

        @pl.when((seen > 0) & (turn < PEERS))
        def _():
            info[2 + turn] = b

        turn = turn + (seen > 0).astype(jnp.int32)
    info[0] = me[0]
    info[1] = turn
    load[0] = turn


def make_plan(me, obs_count):
    blocks = obs_count.shape[0]
    smem = pl.BlockSpec(memory_space=pltpu.SMEM)
    return pl.pallas_call(
        functools.partial(plan_kernel, blocks),
        out_shape=[
            jax.ShapeDtypeStruct((2 + PEERS + blocks,), jnp.int32),
            jax.ShapeDtypeStruct((1,), jnp.int32),
        ],
        in_specs=[smem] * 2,
        out_specs=[smem] * 2,
    )(me, obs_count)


def pack_kernel(nb, base, cols, listed, info, ens, idx, val, rinv, *refs):
    outs, idx_out, val_out, rinv_out, val_all, rinv_all, sems = refs
    slots = idx.shape[1]
    width = nb * cols
    copies = []
    for d in range(PEERS):
        first = info[2 + d] if listed else base + d * nb
        at = pl.multiple_of(first * cols, cols) if listed else first * cols
        copies.append(
            pltpu.make_async_copy(ens.at[:, pl.ds(at, width), :], outs.at[d], sems.at[d])
        )
    for copy in copies:
        copy.start()
    mine = info[2 + info[0]] if listed else base + info[0] * nb
    slot = lax.broadcasted_iota(jnp.int32, (1, slots), 1)
    val_all[...] = val[...].astype(F32)
    rinv_all[...] = rinv[...].astype(F32)
    for q in range(nb):
        row = pl.ds(mine + q, 1)
        idx_out[q : q + 1, :] = idx[row, :]
        val_out[q : q + 1, :] = val_all[row, :]
        used = slot < info[2 + PEERS + mine + q]
        rinv_out[q : q + 1, :] = jnp.where(used, rinv_all[row, :], 0.0)
    for copy in copies:
        copy.wait()


def pack(nb, base, cols, listed, info, ensemble, idx, val, rinv):
    share, _, state = ensemble.shape
    slots = idx.shape[1]
    smem = pl.BlockSpec(memory_space=pltpu.SMEM)
    vmem = pl.BlockSpec(memory_space=pltpu.VMEM)
    hbm = pl.BlockSpec(memory_space=pl.ANY)
    sent, *rows = pl.pallas_call(
        functools.partial(pack_kernel, nb, base, cols, listed),
        out_shape=[
            jax.ShapeDtypeStruct((PEERS, share, nb * cols, state), BF16),
            jax.ShapeDtypeStruct((nb, slots), jnp.int32),
            jax.ShapeDtypeStruct((nb, slots), F32),
            jax.ShapeDtypeStruct((nb, slots), F32),
        ],
        in_specs=[smem, hbm, vmem, vmem, vmem],
        out_specs=[vmem] * 4,
        scratch_shapes=[
            pltpu.VMEM(val.shape, F32),
            pltpu.VMEM(rinv.shape, F32),
            pltpu.SemaphoreType.DMA((PEERS,)),
        ],
        compiler_params=pltpu.CompilerParams(vmem_limit_bytes=16 * 1024 * 1024),
    )(info, ensemble, idx, val, rinv)
    return sent, rows


def all_kernel(*refs):
    chunks, out, sems = refs[:-2], refs[-2], refs[-1]
    copies = []
    for i, chunk in enumerate(chunks):
        width = chunk.shape[2]
        for d in range(PEERS):
            at = (i * PEERS + d) * width
            copies.append(
                pltpu.make_async_copy(
                    chunk.at[d], out.at[:, pl.ds(at, width), :], sems.at[i * PEERS + d]
                )
            )
    for copy in copies:
        copy.start()
    for copy in copies:
        copy.wait()


def still_kernel(info, ens, out, sems):
    blocks = sems.shape[0]
    cols = out.shape[1] // blocks
    copies = []
    for b in range(blocks):
        part = pl.ds(b * cols, cols)
        copies.append((
            info[2 + PEERS + b] <= 0,
            pltpu.make_async_copy(ens.at[:, part, :], out.at[:, part, :], sems.at[b]),
        ))
    for wanted, copy in copies:
        pl.when(wanted)(copy.start)
    for wanted, copy in copies:
        pl.when(wanted)(copy.wait)


def some_kernel(info, held, chunks, out, sems):
    cols = chunks.shape[2]
    copies = []
    for d in range(PEERS):
        at = pl.multiple_of(info[2 + d] * cols, cols)
        copies.append((
            d < info[1],
            pltpu.make_async_copy(chunks.at[d], out.at[:, pl.ds(at, cols), :], sems.at[d]),
        ))
    for wanted, copy in copies:
        pl.when(wanted)(copy.start)
    for wanted, copy in copies:
        pl.when(wanted)(copy.wait)


def assemble(kernel, plans, arrays, chunks, shape, sems, aliases=None):
    hbm = pl.BlockSpec(memory_space=pl.ANY)
    vmem = pl.BlockSpec(memory_space=pltpu.VMEM)
    return pl.pallas_call(
        kernel,
        out_shape=jax.ShapeDtypeStruct(shape, BF16),
        in_specs=[pl.BlockSpec(memory_space=pltpu.SMEM)] * len(plans)
        + [hbm] * len(arrays)
        + [vmem] * len(chunks),
        out_specs=hbm,
        scratch_shapes=[pltpu.SemaphoreType.DMA((sems,))],
        input_output_aliases=aliases or {},
        compiler_params=pltpu.CompilerParams(vmem_limit_bytes=16 * 1024 * 1024),
    )(*plans, *arrays, *chunks)


def shards(ensemble, obs_count, obs_index, obs_value, obs_rinv):
    share, columns, state = ensemble.shape
    blocks = obs_count.shape[0]
    cols = columns // blocks
    me = lax.axis_index("mem").astype(jnp.int32)
    info, load = make_plan(me[None], obs_count)

    def exchange(x):
        return lax.all_to_all(x, "mem", 0, 0, tiled=True)

    def run(nb, base, listed):
        sent, rows = pack(
            nb, base, cols, listed, info, ensemble, obs_index, obs_value, obs_rinv
        )
        return exchange(analyse(nb, cols, *rows, exchange(sent)))

    def whole():
        back = run(blocks // PEERS, 0, False)
        return assemble(all_kernel, [], [], [back], ensemble.shape, PEERS)

    def part():
        sent, rows = pack(
            1, 0, cols, True, info, ensemble, obs_index, obs_value, obs_rinv
        )
        done = analyse(1, cols, *rows, exchange(sent))
        step, done = lax.optimization_barrier((info, done))
        still = assemble(still_kernel, [step], [ensemble], [], ensemble.shape, blocks)
        done, still = lax.optimization_barrier((done, still))
        return assemble(
            some_kernel, [info], [still], [exchange(done)], ensemble.shape, PEERS, {1: 0}
        )

    return lax.cond(load[0] > PEERS, whole, part)


def solution(mesh):
    return jax.shard_map(
        shards,
        mesh=mesh,
        in_specs=(
            P("mem", "space", None),
            P("space"),
            P("space", None),
            P("space", None),
            P("space", None),
        ),
        out_specs=P("mem", "space", None),
        check_vma=False,
    )
```
